256 devices in a mesh: dp: 32 (over y_hi, z, core), ctx: 8 (over x, y_lo).
Axes of the slice: x: 4, y: 4 (y_hi: 2, y_lo: 2; y = y_hi * 2 + y_lo), z: 8, core: 2. Of those that a mesh axis runs over, the one named last changes fastest.
Arguments:
- query_heads: bfloat16 [32, 1024, 4096], P('dp', 'ctx'), may hold values from -160 to 160
- key_heads: bfloat16 [32, 1024, 512], P('dp', 'ctx'), may hold values from -6 to 6
- value_heads: bfloat16 [32, 1024, 512], P('dp', 'ctx'), may hold values from -6 to 6
- out_grad: bfloat16 [32, 1024, 4096], P('dp', 'ctx'), may hold values from -6 to 6
- layer_inputs: bfloat16 [32, 1024, 8192], P('dp', 'ctx'), may hold values from -6 to 6
- doc_lengths: int32 [32, 8], P('dp'), may hold values from 1 to 512, 1024 in all within a row
Outputs:
- query_grad: bfloat16 [32, 1024, 4096], P('dp', 'ctx')
- key_grad: bfloat16 [32, 1024, 512], P('dp', 'ctx')
- value_grad: bfloat16 [32, 1024, 512], P('dp', 'ctx')
- weight_grad: float32 [8192, 512], P(('dp', 'ctx'))
The draws below stay inside these ranges and needn't reach their ends.
All inputs are finite; a program needn't handle non-finite values.
Results may differ from the reference program's by a relative error of at most 0.0053.
Values may be sent and summed in bfloat16 or wider, within the bound.
No kernel may reach another device: no remote copies, remote signals or barrier semaphores. Data moves between devices by JAX's collectives and lax.ppermute only.
A program may use at most 128 MiB of HBM per device.

```python
import math
import jax
import jax.numpy as jnp
import numpy as np
from jax import lax

D = 8192
HD = 128
HEADS = 32
KVH = 4
DOCS = 8
SEQ = 1024
MAXDOC = 512
QW = 4096
KW = 512
N_DP = 32


def shared_keys(key):
    base_keys = jax.random.normal(key, (N_DP, SEQ, KVH, HD), jnp.float32)
    return jnp.clip(base_keys, -6.0, 6.0)


def draw_key_heads(key, part):
    base_keys = shared_keys(key)
    return base_keys.reshape(N_DP, SEQ, KVH * HD).astype(jnp.bfloat16)


def draw_query_heads(key, part):
    key = jax.random.fold_in(key, 7)
    group_size = HEADS // KVH
    draw_shape = (N_DP, SEQ, KVH, group_size, HD)
    entries = jnp.clip(jax.random.normal(key, draw_shape, jnp.float32), -6.0, 6.0)
    return entries.reshape(N_DP, SEQ, HEADS * HD).astype(jnp.bfloat16)


def spiked(values, key, source, target, parts, factor):
    def block_of(dim):
        return (jnp.arange(values.shape[dim]) // (values.shape[dim] // parts)).reshape((-1,) + (1,) * (values.ndim - 1 - dim))

    one_side = jax.random.permutation(key, parts)[block_of(target)]
    second = (block_of(target) + parts // 2) % parts
    return jnp.where((block_of(source) == one_side) | (block_of(source) == second), factor * values, values)


def shard_levels(stream_key, dims, pieces, low, largest):
    gain, own = 1.0, jax.random.fold_in(stream_key, 6)
    for position, shards_of in pieces:
        steps = jnp.exp(jax.random.uniform(jax.random.fold_in(own, position), (shards_of,), jnp.float32, low / len(pieces), largest / len(pieces)))
        gain = gain * jnp.repeat(steps, dims[position] // shards_of).reshape([-1 if axis == position else 1 for axis in range(len(dims))])
    return gain


def profile(count, total, most, slope):
    portions = [(1 << 20) // math.isqrt(grade ** slope) + 1 for grade in range(2, count + 1)]
    surplus, given = total - most - (count - 1), [1] * (count - 1)
    while surplus > 0:
        free = [i for i in range(count - 1) if given[i] < most]
        mass, budget = sum([portions[i] for i in free]), surplus
        for i in free:
            more = min(most - given[i], max(1, budget * portions[i] // mass), surplus)
            given[i] = given[i] + more
            surplus = surplus - more
    return np.array([most] + given)


def ragged_sizes(stream_key, number_of, total, reach, skew):
    if number_of == 2:
        one = jax.random.randint(stream_key, (), max(1, total - reach), min(reach, total - 1) + 1)
        return jnp.stack([one, total - one])
    tallies = jnp.asarray(profile(number_of, total, reach, skew), jnp.int32)
    couples = (number_of - 1) // 2
    giver, receiver = tallies[1:1 + 2 * couples:2], tallies[2:2 + 2 * couples:2]
    slack = jnp.minimum(giver - 1, reach - receiver)
    moved = jax.random.randint(jax.random.fold_in(stream_key, 1), (couples,), 0, 1 << 20) % (slack + 1)
    tallies = tallies.at[1:1 + 2 * couples:2].set(giver - moved).at[2:2 + 2 * couples:2].set(receiver + moved)
    return tallies[jax.random.permutation(jax.random.fold_in(stream_key, 2), number_of)]


def centred(key, dims, spread, bound, pieces=(), kind=jnp.bfloat16):
    loudness = shard_levels(key, dims, pieces, -0.22, 0.18) if pieces else 1.0
    result = jax.random.normal(key, dims, jnp.float32) * spread * loudness
    return jnp.minimum(jnp.maximum(result, -bound), bound).astype(kind)


def bell_draw_with(rng, dims, spread, most, cuts, heavy, held_as=jnp.bfloat16):
    drawn = spread * jax.random.normal(rng, dims, jnp.float32)
    if cuts:
        drawn = drawn * shard_levels(rng, dims, cuts, -0.22, 0.18)
    return jnp.clip(spiked(drawn, jax.random.fold_in(rng, 3), *heavy), -most, most).astype(held_as)


def setup_inputs(seed: int = 0) -> dict:
    streams_of = jax.random.split(jax.random.key(seed), 7)
    return {
        "query_heads": draw_query_heads(jax.random.fold_in(streams_of[6], 71), 0),
        "key_heads": draw_key_heads(jax.random.fold_in(streams_of[6], 71), 0),
        "value_heads": centred(streams_of[2], (N_DP, SEQ, KW), 1.0, 6.0, ((0, 32), (1, 8))),
        "out_grad": centred(streams_of[3], (N_DP, SEQ, QW), 1.0, 6.0, ((0, 32), (1, 8))),
        "layer_inputs": bell_draw_with(streams_of[4], (N_DP, SEQ, D), 1.0, 6.0, ((0, 32), (1, 8)), (0, 2, 32, 2.75)),
        "doc_lengths": jax.vmap(lambda own: ragged_sizes(own, DOCS, SEQ, MAXDOC, 2))(jax.random.split(streams_of[5], N_DP)).reshape((N_DP, DOCS)).astype(jnp.int32),
    }


NEG_FILL = -1e30


def document_ids(lengths_row, length):
    endings = jnp.cumsum(lengths_row).astype(jnp.int32)
    positions = jnp.arange(length, dtype=jnp.int32)
    return jnp.sum((positions[:, None] >= endings[None, :]).astype(jnp.int32), axis=1)


def one_sequence(packed):
    query_rows, key_rows, value_rows, grad_rows, lengths_row = packed
    length = query_rows.shape[0]
    group_size = HEADS // KVH
    softmax_scale = HD ** -0.5
    query_split = query_rows.reshape(length, KVH, group_size, HD).astype(jnp.float32)
    key_split = key_rows.reshape(length, KVH, HD).astype(jnp.float32)
    value_split = value_rows.reshape(length, KVH, HD).astype(jnp.float32)
    grad_split = grad_rows.reshape(length, KVH, group_size, HD).astype(jnp.float32)
    documents = document_ids(lengths_row, length)
    positions = jnp.arange(length, dtype=jnp.int32)
    allowed = (documents[:, None] == documents[None, :]) & (positions[None, :] <= positions[:, None])
    scores = jnp.einsum("igsd,jgd->gsij", query_split, key_split) * softmax_scale
    scores = jnp.where(allowed[None, None], scores, NEG_FILL)
    row_top = jnp.max(scores, axis=-1, keepdims=True)
    row_total = jnp.sum(jnp.exp(scores - row_top), axis=-1, keepdims=True)
    row_lse = row_top + jnp.log(row_total)
    probability = jnp.exp(scores - row_lse)
    prob_low = lax.optimization_barrier(probability.astype(jnp.bfloat16)).astype(jnp.float32)
    attended = jnp.einsum("gsij,jgd->igsd", prob_low, value_split)
    delta = jnp.transpose(jnp.sum(grad_split * attended, axis=-1), (1, 2, 0))
    dprob = jnp.einsum("igsd,jgd->gsij", grad_split, value_split)
    dscore = probability * (dprob - delta[..., None])
    dscore_low = lax.optimization_barrier(dscore.astype(jnp.bfloat16)).astype(jnp.float32)
    query_grad = jnp.einsum("gsij,jgd->igsd", dscore_low, key_split) * softmax_scale
    key_grad = jnp.einsum("gsij,igsd->jgd", dscore_low, query_split) * softmax_scale
    value_grad = jnp.einsum("gsij,igsd->jgd", prob_low, grad_split)
    return (query_grad.reshape(length, HEADS * HD).astype(jnp.bfloat16),
            key_grad.reshape(length, KVH * HD).astype(jnp.bfloat16),
            value_grad.reshape(length, KVH * HD).astype(jnp.bfloat16))


def reference(query_heads, key_heads, value_heads, out_grad, layer_inputs, doc_lengths):
    query_grad, key_grad, value_grad = lax.map(one_sequence, (query_heads, key_heads, value_heads, out_grad, doc_lengths))
    width = layer_inputs.shape[2]
    key_width = key_heads.shape[2]

    def add_sequence(running, pair):
        input_rows, grad_rows = pair
        term = jnp.dot(input_rows.T, grad_rows, preferred_element_type=jnp.float32)
        return running + term, None

    start_grad = jnp.zeros((width, key_width), jnp.float32)
    weight_grad, unused_rest = lax.scan(add_sequence, start_grad, (layer_inputs, value_grad))
    token_total = layer_inputs.shape[0] * layer_inputs.shape[1]
    weight_grad = weight_grad * (token_total ** -0.5)
    return (query_grad, key_grad, value_grad, weight_grad)
```

```python
import math

import jax
import jax.numpy as jnp
from jax import lax
from jax.experimental import pallas as pl
from jax.experimental.pallas import tpu as pltpu
from jax.sharding import PartitionSpec as P

HD = 128
GROUPS = 4
GROUP = 8
ROWS = 128
NEAR = 4
SCALE = HD**-0.5
SCALE_LOG2 = SCALE * math.log2(math.e)
NEG_FILL = -1e30
F32 = jnp.float32
BF16 = jnp.bfloat16


def params(mib):
    return pltpu.CompilerParams(vmem_limit_bytes=mib * 2**20)


def dot(a, b, contract):
    return lax.dot_general(a, b, ((contract[:1], contract[1:]), ((), ())), preferred_element_type=F32)


def fill_bias(lengths, bias):
    first = lax.axis_index("ctx") * ROWS
    query = lax.broadcasted_iota(jnp.int32, (ROWS, 2 * ROWS), 1) % ROWS
    key = lax.broadcasted_iota(jnp.int32, (ROWS, 2 * ROWS), 0)
    start = jnp.zeros_like(query)
    ending = jnp.int32(0)
    for n in range(lengths.shape[1]):
        ending = ending + lengths[0, n]
        start = jnp.where(ending <= query + first, ending, start)
    for block in range(NEAR):
        place = key + (first - block * ROWS)
        if block == 0:
            place = jnp.where(key <= query, place, place - NEAR * ROWS)
        bias[block * ROWS : (block + 1) * ROWS, :] = jnp.where(place >= start, 0.0, NEG_FILL)


def lower():
    query = lax.broadcasted_iota(jnp.int32, (ROWS, 2 * ROWS), 1) % ROWS
    key = lax.broadcasted_iota(jnp.int32, (ROWS, 2 * ROWS), 0)
    return key <= query


def fold(tile, mask):
    return jnp.concatenate(
        [jnp.where(mask, tile[:ROWS], tile[NEAR * ROWS :]), tile[ROWS : NEAR * ROWS]], axis=0
    )


def unfold(tile, mask):
    return jnp.concatenate(
        [
            jnp.where(mask, tile[:ROWS], 0.0).astype(BF16),
            tile[ROWS:].astype(BF16),
            jnp.where(mask, 0.0, tile[:ROWS]).astype(BF16),
        ],
        axis=0,
    )


def heads(ref, first, count):
    return jnp.concatenate([ref[:, (first + n) * HD : (first + n + 1) * HD] for n in range(count)], axis=0)


def value_kernel(lengths, q, do, k0, k1, k2, k3, k4, own, s1, s2, s3, s4, stats, bias, prob):
    @pl.when(pl.program_id(0) == 0)
    def _():
        fill_bias(lengths, bias)

    mask = lower()
    keys = jnp.concatenate([ref[...] for ref in (k0, k1, k2, k3, k4)], axis=0)
    for pair in range(GROUP // 2):
        lanes = slice(pair * 256, (pair + 1) * 256)
        scores = fold(dot(keys, heads(q, 2 * pair, 2), (1, 1)), mask) + bias[...]
        top = jnp.max(scores, axis=0, keepdims=True)
        weight = jnp.exp2((scores - top) * SCALE_LOG2)
        inverse = 1.0 / jnp.sum(weight, axis=0, keepdims=True)
        prob[:, lanes] = unfold(weight * inverse, mask)
        stats[0, 0:1, lanes] = top
        stats[0, 1:2, lanes] = inverse
    grad = dot(prob[...], heads(do, 0, GROUP), (1, 0))
    own[...] = grad[:ROWS]
    for n, ref in enumerate((s1, s2, s3, s4)):
        ref[...] = grad[(n + 1) * ROWS : (n + 2) * ROWS].astype(BF16)


def score_kernel(
    lengths, q, do, k0, k1, k2, k3, k4, v0, v1, v2, v3, v4, stats, dq, own, s1, s2, s3, s4, bias, dsc
):
    @pl.when(pl.program_id(0) == 0)
    def _():
        fill_bias(lengths, bias)

    mask = lower()
    keys = jnp.concatenate([ref[...] for ref in (k0, k1, k2, k3, k4)], axis=0)
    values = jnp.concatenate([ref[...] for ref in (v0, v1, v2, v3, v4)], axis=0)
    keys_t = jnp.concatenate([ref[...].T for ref in (k0, k1, k2, k3, k4)], axis=1)
    for pair in range(GROUP // 2):
        lanes = slice(pair * 256, (pair + 1) * 256)
        top, inverse = stats[0, 0:1, lanes], stats[0, 1:2, lanes]
        scores = fold(dot(keys, heads(q, 2 * pair, 2), (1, 1)), mask) + bias[...]
        probability = jnp.exp2((scores - top) * SCALE_LOG2) * inverse
        dprob = fold(dot(values, heads(do, 2 * pair, 2), (1, 1)), mask)
        delta = jnp.sum(probability.astype(BF16).astype(F32) * dprob, axis=0, keepdims=True)
        low = unfold(probability * (dprob - delta), mask)
        dsc[:, lanes] = low
        dq_t = dot(keys_t, low, (1, 0)) * SCALE
        for n in range(2):
            cols = slice((2 * pair + n) * HD, (2 * pair + n + 1) * HD)
            dq[:, cols] = dq_t[:, n * HD : (n + 1) * HD].T.astype(BF16)
    grad = dot(dsc[...], heads(q, 0, GROUP), (1, 0)) * SCALE
    own[...] = grad[:ROWS]
    for n, ref in enumerate((s1, s2, s3, s4)):
        ref[...] = grad[(n + 1) * ROWS : (n + 2) * ROWS].astype(BF16)


def group_spec(width):
    return pl.BlockSpec((ROWS, width), lambda g: (0, g))


def whole_spec(shape):
    return pl.BlockSpec(shape, lambda *_: (0,) * len(shape))


STATS_SPEC = pl.BlockSpec((1, 8, GROUP * ROWS), lambda g: (g, 0, 0))
SMEM = pl.BlockSpec(memory_space=pltpu.SMEM)


def sds(shape, dtype):
    return jax.ShapeDtypeStruct(shape, dtype)


def value_call(lengths, q, do, keys):
    key_spec = group_spec(HD)
    width = GROUPS * HD
    return pl.pallas_call(
        value_kernel,
        grid=(GROUPS,),
        in_specs=[SMEM, group_spec(GROUP * HD), group_spec(GROUP * HD)] + [key_spec] * 5,
        out_specs=[key_spec] * 5 + [STATS_SPEC],
        out_shape=[sds((ROWS, width), F32)]
        + [sds((ROWS, width), BF16)] * NEAR
        + [sds((GROUPS, 8, GROUP * ROWS), F32)],
        scratch_shapes=[
            pltpu.VMEM((NEAR * ROWS, 2 * ROWS), F32),
            pltpu.VMEM((5 * ROWS, GROUP * ROWS), BF16),
        ],
        compiler_params=params(32),
        cost_estimate=pl.CostEstimate(flops=10**10, bytes_accessed=4 * 10**6, transcendentals=2 * 10**6),
        name="value_grad",
    )(lengths, q, do, *keys)


def score_call(lengths, q, do, keys, values, stats):
    key_spec = group_spec(HD)
    width = GROUPS * HD
    return pl.pallas_call(
        score_kernel,
        grid=(GROUPS,),
        in_specs=[SMEM, group_spec(GROUP * HD), group_spec(GROUP * HD)] + [key_spec] * 10 + [STATS_SPEC],
        out_specs=[group_spec(GROUP * HD)] + [key_spec] * 5,
        out_shape=[sds((ROWS, GROUPS * GROUP * HD), BF16), sds((ROWS, width), F32)]
        + [sds((ROWS, width), BF16)] * NEAR,
        scratch_shapes=[
            pltpu.VMEM((NEAR * ROWS, 2 * ROWS), F32),
            pltpu.VMEM((5 * ROWS, GROUP * ROWS), BF16),
        ],
        compiler_params=params(32),
        cost_estimate=pl.CostEstimate(flops=10**10, bytes_accessed=4 * 10**6, transcendentals=2 * 10**6),
        name="score_grad",
    )(lengths, q, do, *keys, *values, stats)


def deal_kernel(x, *refs):
    outs, pick = refs[:8], refs[8]
    dp, ctx = lax.axis_index("dp"), lax.axis_index("ctx")
    core, high = dp % 2, dp // 16

    @pl.when(pl.program_id(0) == 0)
    def _():
        row = lax.broadcasted_iota(jnp.int32, (1024, 1024), 0)
        col = lax.broadcasted_iota(jnp.int32, (1024, 1024), 1)
        to, far, pair, n = row // 128, (row // 64) % 2, (row // 32) % 2, row % 32
        source = (pair * 2 + (far ^ core)) * 256 + ((to + ctx) % 8) * 32 + n
        pick[...] = jnp.where(col == source, 1.0, 0.0).astype(BF16)

    step = pl.program_id(0)
    dealt = dot(pick[...], x[...], (1, 1)).astype(BF16)
    for to in range(8):
        outs[to][0] = dealt[to * 128 : to * 128 + 64]
        outs[to][1] = dealt[to * 128 + 64 : to * 128 + 128]


def deal_call(x):
    def source(step):
        return (0, step ^ (4 * (lax.axis_index("dp") // 16)))

    return pl.pallas_call(
        deal_kernel,
        grid=(8,),
        in_specs=[pl.BlockSpec((ROWS, 1024), source)],
        out_specs=[pl.BlockSpec((2, 64, ROWS), lambda step: (0, step, 0))] * 8,
        out_shape=[sds((2, 512, ROWS), BF16)] * 8,
        scratch_shapes=[pltpu.VMEM((1024, 1024), BF16)],
        compiler_params=params(24),
        cost_estimate=pl.CostEstimate(flops=2 * 10**9, bytes_accessed=4 * 10**6, transcendentals=0),
        name="deal_inputs",
    )(x)


def weight_kernel(*refs):
    inputs, grads, out = refs[:8], refs[8:16], refs[16]
    left = jnp.concatenate([ref[0] for ref in inputs], axis=1)
    right = jnp.concatenate([ref[...] for ref in grads], axis=0)
    out[...] = dot(left, right, (1, 0)).astype(out.dtype)


def weight_call(half, inputs, grads, dtype):
    width = grads[0].shape[1]
    return pl.pallas_call(
        weight_kernel,
        grid=(2,),
        in_specs=[pl.BlockSpec((1, 256, ROWS), lambda n: (half, n, 0))] * 8 + [whole_spec((ROWS, width))] * 8,
        out_specs=pl.BlockSpec((256, width), lambda n: (n, 0)),
        out_shape=sds((512, width), dtype),
        compiler_params=params(24),
        cost_estimate=pl.CostEstimate(flops=6 * 10**8, bytes_accessed=3 * 10**6, transcendentals=0),
        name="weight_grad",
    )(*inputs, *grads)


def send(array, axis, target, count):
    return lax.ppermute(array, axis, [(n, target(n)) for n in range(count)])


def ring(array, distance):
    return send(array, "ctx", lambda n: (n + distance) % 8, 8)


def after(array, *others):
    return lax.optimization_barrier((array, *others))[0]


def shards(query_heads, key_heads, value_heads, out_grad, layer_inputs, doc_lengths):
    q, do = query_heads[0], out_grad[0]
    key, value = key_heads[0], value_heads[0]
    tokens = lax.axis_size("dp") * lax.axis_size("ctx") * q.shape[0]
    keys = [key] + [ring(key, d) for d in range(1, 5)]
    dealt = deal_call(layer_inputs[0])
    values = [value] + [ring(value, d) for d in range(1, 5)]
    inputs = [dealt[0]] + [ring(dealt[d], d) for d in range(1, 8)]

    *value_terms, stats = value_call(doc_lengths, q, do, keys)
    arrived = [ring(term, -d) for d, term in enumerate(value_terms[1:], 1)]
    value_grad = (value_terms[0] + sum(term.astype(F32) for term in arrived)).astype(BF16)
    query_grad, *key_terms = score_call(doc_lengths, q, do, keys, values, stats)

    grads = [value_grad] + [ring(value_grad, d) for d in range(1, 8)]
    away = weight_call(1, inputs, grads, BF16)
    other_core = send(away, "dp", lambda n: n ^ 1, 32)
    here = weight_call(0, inputs, grads, F32)
    total = here + other_core.astype(F32)
    other_high = send(total[256:].astype(BF16), "dp", lambda n: n ^ 16, 32)
    total = total[:256] + other_high.astype(F32)
    rings = [[high * 16 + 2 * z + core for z in range(8)] for high in range(2) for core in range(2)]
    parts = lax.all_to_all(total.astype(BF16).reshape(8, 32, -1), "dp", 0, 0, axis_index_groups=rings)
    weight_grad = jnp.sum(parts.astype(F32), axis=0) * tokens**-0.5

    arrived = [ring(term, -d) for d, term in enumerate(key_terms[1:], 1)]
    key_grad = (key_terms[0] + sum(term.astype(F32) for term in arrived)).astype(BF16)
    return query_grad[None], key_grad[None], value_grad[None], weight_grad


def solution(mesh):
    split = P("dp", "ctx", None)
    return jax.shard_map(
        shards,
        mesh=mesh,
        in_specs=(split,) * 5 + (P("dp", None),),
        out_specs=(split, split, split, P(("dp", "ctx"), None)),
        check_vma=False,
    )
```

```python
import functools
import math

import jax
import jax.numpy as jnp
from jax import lax
from jax.experimental import pallas as pl
from jax.experimental.pallas import tpu as pltpu
from jax.sharding import PartitionSpec as P

HD = 128
GROUPS = 4
GROUP = 8
ROWS = 128
NEAR = 4
SCALE = HD**-0.5
SCALE_LOG2 = SCALE * math.log2(math.e)
NEG_FILL = -1e30
F32 = jnp.float32
BF16 = jnp.bfloat16


def params(mib):
    return pltpu.CompilerParams(vmem_limit_bytes=mib * 2**20)


def dot(a, b, contract):
    return lax.dot_general(a, b, ((contract[:1], contract[1:]), ((), ())), preferred_element_type=F32)


def fill_bias(lengths, bias):
    first = lax.axis_index("ctx") * ROWS
    query = lax.broadcasted_iota(jnp.int32, (ROWS, 2 * ROWS), 1) % ROWS
    key = lax.broadcasted_iota(jnp.int32, (ROWS, 2 * ROWS), 0)
    start = jnp.zeros_like(query)
    ending = jnp.int32(0)
    for n in range(lengths.shape[1]):
        ending = ending + lengths[0, n]
        start = jnp.where(ending <= query + first, ending, start)
    for block in range(NEAR):
        place = key + (first - block * ROWS)
        if block == 0:
            place = jnp.where(key <= query, place, place - NEAR * ROWS)
        bias[block * ROWS : (block + 1) * ROWS, :] = jnp.where(place >= start, 0.0, NEG_FILL)


def lower():
    query = lax.broadcasted_iota(jnp.int32, (ROWS, 2 * ROWS), 1) % ROWS
    key = lax.broadcasted_iota(jnp.int32, (ROWS, 2 * ROWS), 0)
    return key <= query


def fold(tile, mask):
    return jnp.concatenate(
        [jnp.where(mask, tile[:ROWS], tile[NEAR * ROWS :]), tile[ROWS : NEAR * ROWS]], axis=0
    )


def unfold(tile, mask):
    return jnp.concatenate(
        [
            jnp.where(mask, tile[:ROWS], 0.0).astype(BF16),
            tile[ROWS:].astype(BF16),
            jnp.where(mask, 0.0, tile[:ROWS]).astype(BF16),
        ],
        axis=0,
    )


def heads(ref, first, count):
    return jnp.concatenate([ref[:, (first + n) * HD : (first + n + 1) * HD] for n in range(count)], axis=0)


def blocks(refs, column):
    return jnp.concatenate([ref[:, column * HD : (column + 1) * HD] for ref in refs], axis=0)


def hand_out(grad, group, outs):
    cols = slice(group * HD, (group + 1) * HD)
    for n, ref in enumerate(outs):
        ref[:, cols] = grad[n * ROWS : (n + 1) * ROWS].astype(ref.dtype)


def value_kernel(lengths, q, do, k0, k1, k2, k3, k4, own, s1, s2, s3, s4, stats, bias, prob):
    fill_bias(lengths, bias)
    mask = lower()
    for group in range(GROUPS):
        keys = blocks((k0, k1, k2, k3, k4), group)
        for pair in range(GROUP // 2):
            lanes = slice(pair * 256, (pair + 1) * 256)
            scores = fold(dot(keys, heads(q, group * GROUP + 2 * pair, 2), (1, 1)), mask) + bias[...]
            top = jnp.max(scores, axis=0, keepdims=True)
            weight = jnp.exp2((scores - top) * SCALE_LOG2)
            inverse = 1.0 / jnp.sum(weight, axis=0, keepdims=True)
            prob[group % 2, :, lanes] = unfold(weight * inverse, mask)
            stats[group, 0:1, lanes] = top
            stats[group, 1:2, lanes] = inverse
        grad = dot(prob[group % 2], heads(do, group * GROUP, GROUP), (1, 0))
        hand_out(grad, group, (own, s1, s2, s3, s4))


def score_kernel(
    lengths, q, do, k0, k1, k2, k3, k4, v0, v1, v2, v3, v4, stats, dq, own, s1, s2, s3, s4, bias, dsc
):
    fill_bias(lengths, bias)
    mask = lower()
    for group in range(GROUPS):
        keys, values = blocks((k0, k1, k2, k3, k4), group), blocks((v0, v1, v2, v3, v4), group)
        for pair in range(GROUP // 2):
            lanes = slice(pair * 256, (pair + 1) * 256)
            first = group * GROUP + 2 * pair
            top, inverse = stats[group, 0:1, lanes], stats[group, 1:2, lanes]
            scores = fold(dot(keys, heads(q, first, 2), (1, 1)), mask) + bias[...]
            probability = jnp.exp2((scores - top) * SCALE_LOG2) * inverse
            dprob = fold(dot(values, heads(do, first, 2), (1, 1)), mask)
            delta = jnp.sum(probability.astype(BF16).astype(F32) * dprob, axis=0, keepdims=True)
            dsc[group % 2, :, lanes] = unfold(probability * (dprob - delta), mask)
        rows = (dot(dsc[group % 2], keys, (0, 0)) * SCALE).astype(BF16)
        for n in range(GROUP):
            head = group * GROUP + n
            dq[:, head * HD : (head + 1) * HD] = rows[n * HD : (n + 1) * HD]
        grad = dot(dsc[group % 2], heads(q, group * GROUP, GROUP), (1, 0)) * SCALE
        hand_out(grad, group, (own, s1, s2, s3, s4))


def sds(shape, dtype):
    return jax.ShapeDtypeStruct(shape, dtype)


VMEM = pl.BlockSpec(memory_space=pltpu.VMEM)
SMEM = pl.BlockSpec(memory_space=pltpu.SMEM)
TERMS = [sds((ROWS, GROUPS * HD), F32)] + [sds((ROWS, GROUPS * HD), BF16)] * NEAR
STATS = sds((GROUPS, 8, GROUP * ROWS), F32)
SCRATCH = [pltpu.VMEM((NEAR * ROWS, 2 * ROWS), F32), pltpu.VMEM((2, 5 * ROWS, GROUP * ROWS), BF16)]


def value_call(lengths, q, do, keys):
    return pl.pallas_call(
        value_kernel,
        in_specs=[SMEM] + [VMEM] * 7,
        out_specs=[VMEM] * 6,
        out_shape=TERMS + [STATS],
        scratch_shapes=SCRATCH,
        compiler_params=params(58),
        cost_estimate=pl.CostEstimate(flops=3 * 10**10, bytes_accessed=4 * 10**6, transcendentals=2 * 10**6),
        name="value_grad",
    )(lengths, q, do, *keys)


def score_call(lengths, q, do, keys, values, stats):
    return pl.pallas_call(
        score_kernel,
        in_specs=[SMEM] + [VMEM] * 13,
        out_specs=[VMEM] * 6,
        out_shape=[sds((ROWS, GROUPS * GROUP * HD), BF16)] + TERMS,
        scratch_shapes=SCRATCH,
        compiler_params=params(58),
        cost_estimate=pl.CostEstimate(flops=4 * 10**10, bytes_accessed=4 * 10**6, transcendentals=2 * 10**6),
        name="score_grad",
    )(lengths, q, do, *keys, *values, stats)


def deal_kernel(x, out, pick):
    step = pl.program_id(0)

    @pl.when(step == 0)
    def _():
        row = lax.broadcasted_iota(jnp.int32, (256, 256), 0)
        col = lax.broadcasted_iota(jnp.int32, (256, 256), 1)
        pick[...] = jnp.where(row == col, 1.0, 0.0).astype(BF16)

    for n in range(4):
        dealt = dot(pick[...], x[:, n * 256 : (n + 1) * 256], (1, 1)).astype(BF16)
        member = (n % 2) * 4 + (step // 4) * 2 + n // 2
        for ctx in range(8):
            first = pl.multiple_of((ctx % 2) * 128 + (step % 4) * 32, 32)
            out[member, ctx // 2, pl.ds(first, 32)] = dealt[ctx * 32 : (ctx + 1) * 32]


def deal_call(x):
    return pl.pallas_call(
        deal_kernel,
        grid=(8,),
        in_specs=[pl.BlockSpec((ROWS, 1024), lambda step: (0, step))],
        out_specs=pl.BlockSpec((8, 4, 256, ROWS), lambda step: (0, 0, 0, 0)),
        out_shape=sds((8, 4, 256, ROWS), BF16),
        scratch_shapes=[pltpu.VMEM((256, 256), BF16)],
        compiler_params=params(24),
        cost_estimate=pl.CostEstimate(flops=2 * 10**9, bytes_accessed=4 * 10**6, transcendentals=0),
        name="deal_inputs",
    )(x)


def weight_kernel(first, inputs, *refs):
    grads, outs = refs[:8], refs[8:]
    dp, ctx = lax.axis_index("dp"), lax.axis_index("ctx")
    core, high, low, x = dp % 2, dp // 16, dp // 2 % 2, ctx // 2
    members = [(core ^ c) * 4 + (high ^ h) * 2 + (low ^ n) for c in range(2) for n in range(2) for h in range(2)]
    right = jnp.concatenate([ref[...] for ref in grads], axis=0)
    for n, out in enumerate(outs):
        left = jnp.concatenate([inputs[member, (x + first + n) % 4] for member in members], axis=1)
        out[...] = dot(left, right, (1, 0)).astype(out.dtype)


def weight_call(first, count, inputs, grads, dtype):
    width = grads[0].shape[1]
    return pl.pallas_call(
        functools.partial(weight_kernel, first),
        in_specs=[VMEM] * 9,
        out_specs=[VMEM] * count,
        out_shape=[sds((256, width), dtype)] * count,
        compiler_params=params(24),
        cost_estimate=pl.CostEstimate(flops=3 * 10**8 * count, bytes_accessed=10**6 * count, transcendentals=0),
        name="weight_grad",
    )(inputs, *grads)


def place(device):
    dp, ctx = divmod(device, 8)
    return ctx // 2, dp // 16 * 2 + ctx % 2, dp // 2 % 8, dp % 2


def device(x, y, z, core):
    return ((y // 2 * 8 + z) * 2 + core) * 8 + x * 2 + y % 2


def move(array, dx=0, flip_y=False, flip_z=False, flip_core=False):
    pairs = []
    for source in range(256):
        x, y, z, core = place(source)
        target = device((x + dx) % 4, 3 - y if flip_y else y, z ^ flip_z, core ^ flip_core)
        pairs.append((source, target))
    return lax.ppermute(array, ("dp", "ctx"), pairs)


def ring(array, distance):
    return lax.ppermute(array, "ctx", [(n, (n + distance) % 8) for n in range(8)])


def after(array, *others):
    return lax.optimization_barrier((array, *others))[0]


def shards(query_heads, key_heads, value_heads, out_grad, layer_inputs, doc_lengths):
    q, do = query_heads[0], out_grad[0]
    key, value = key_heads[0], value_heads[0]
    tokens = lax.axis_size("dp") * lax.axis_size("ctx") * q.shape[0]
    keys = [key] + [ring(key, d) for d in range(1, 5)]
    values = [value] + [ring(value, d) for d in range(1, 5)]
    dealt = deal_call(layer_inputs[0])
    members = [
        [device(x, y, z, core) for core in range(2) for y in ys for z in (z0, z0 + 1)]
        for x in range(4)
        for ys in ((1, 2), (0, 3))
        for z0 in range(0, 8, 2)
    ]
    inputs = lax.all_to_all(dealt, ("dp", "ctx"), 0, 0, axis_index_groups=members)

    *value_terms, stats = value_call(doc_lengths, q, do, keys)
    arrived = [ring(term, -d) for d, term in enumerate(value_terms[1:], 1)]
    value_grad = (after(value_terms[0], *values) + sum(term.astype(F32) for term in arrived)).astype(BF16)

    flips = ((True, False), (False, True), (True, True))
    grads = [value_grad] + [move(value_grad, flip_y=y, flip_z=z) for y, z in flips]
    grads += [move(grad, flip_core=True) for grad in grads]
    away = weight_call(1, 3, inputs, grads, BF16)
    across = [move(term, dx=d) for d, term in enumerate(away, 1)]
    (total,) = weight_call(0, 1, inputs, grads, F32)

    query_grad, *key_terms = score_call(doc_lengths, q, do, keys, values, after(stats, total))
    arrived = [ring(term, -d) for d, term in enumerate(key_terms[1:], 1)]
    key_grad = (key_terms[0] + sum(term.astype(F32) for term in arrived)).astype(BF16)
    total = (after(total, query_grad) + sum(term.astype(F32) for term in across)).astype(BF16)
    owners = [
        [device(x, 2 * high + y, 2 * z + low, core) for y in range(2) for z in range(4)]
        for x in range(4)
        for high in range(2)
        for low in range(2)
        for core in range(2)
    ]
    parts = lax.all_to_all(total.reshape(8, 32, -1), ("dp", "ctx"), 0, 0, axis_index_groups=owners)
    weight_grad = jnp.sum(parts.astype(F32), axis=0) * tokens**-0.5

    return query_grad[None], key_grad[None], value_grad[None], weight_grad


def solution(mesh):
    split = P("dp", "ctx", None)
    return jax.shard_map(
        shards,
        mesh=mesh,
        in_specs=(split,) * 5 + (P("dp", None),),
        out_specs=(split, split, split, P(("dp", "ctx"), None)),
        check_vma=False,
    )
```

```python
import functools
import math

import jax
import jax.numpy as jnp
from jax import lax
from jax.experimental import pallas as pl
from jax.experimental.pallas import tpu as pltpu
from jax.sharding import PartitionSpec as P

HD = 128
GROUPS = 4
GROUP = 8
ROWS = 128
NEAR = 4
SCALE = HD**-0.5
SCALE_LOG2 = SCALE * math.log2(math.e)
NEG_FILL = -1e30
F32 = jnp.float32
BF16 = jnp.bfloat16


def params(mib):
    return pltpu.CompilerParams(vmem_limit_bytes=mib * 2**20)


def dot(a, b, contract):
    return lax.dot_general(a, b, ((contract[:1], contract[1:]), ((), ())), preferred_element_type=F32)


def fill_bias(lengths, bias):
    first = lax.axis_index("ctx") * ROWS
    query = lax.broadcasted_iota(jnp.int32, (ROWS, 2 * ROWS), 1) % ROWS
    key = lax.broadcasted_iota(jnp.int32, (ROWS, 2 * ROWS), 0)
    start = jnp.zeros_like(query)
    ending = jnp.int32(0)
    for n in range(lengths.shape[1]):
        ending = ending + lengths[0, n]
        start = jnp.where(ending <= query + first, ending, start)
    for block in range(NEAR):
        place = key + (first - block * ROWS)
        if block == 0:
            place = jnp.where(key <= query, place, place - NEAR * ROWS)
        bias[block * ROWS : (block + 1) * ROWS, :] = jnp.where(place >= start, 0.0, NEG_FILL)


def lower():
    query = lax.broadcasted_iota(jnp.int32, (ROWS, 2 * ROWS), 1) % ROWS
    key = lax.broadcasted_iota(jnp.int32, (ROWS, 2 * ROWS), 0)
    return key <= query


def fold(tile, mask):
    return jnp.concatenate(
        [jnp.where(mask, tile[:ROWS], tile[NEAR * ROWS :]), tile[ROWS : NEAR * ROWS]], axis=0
    )


def unfold(tile, mask):
    return jnp.concatenate(
        [
            jnp.where(mask, tile[:ROWS], 0.0).astype(BF16),
            tile[ROWS:].astype(BF16),
            jnp.where(mask, 0.0, tile[:ROWS]).astype(BF16),
        ],
        axis=0,
    )


def heads(ref, first, count):
    return jnp.concatenate([ref[:, (first + n) * HD : (first + n + 1) * HD] for n in range(count)], axis=0)


def blocks(refs, column):
    return jnp.concatenate([ref[:, column * HD : (column + 1) * HD] for ref in refs], axis=0)


def hand_out(grad, group, outs):
    cols = slice(group * HD, (group + 1) * HD)
    for n, ref in enumerate(outs):
        ref[:, cols] = grad[n * ROWS : (n + 1) * ROWS].astype(ref.dtype)


def value_kernel(lengths, value, q, do, k0, k1, k2, k3, k4, passed, own, s1, s2, s3, s4, stats, bias, prob):
    passed[...] = value[...]
    fill_bias(lengths, bias)
    mask = lower()
    for group in range(GROUPS):
        keys = blocks((k0, k1, k2, k3, k4), group)
        for pair in range(GROUP // 2):
            lanes = slice(pair * 256, (pair + 1) * 256)
            scores = fold(dot(keys, heads(q, group * GROUP + 2 * pair, 2), (1, 1)), mask) + bias[...]
            top = jnp.max(scores, axis=0, keepdims=True)
            weight = jnp.exp2((scores - top) * SCALE_LOG2)
            inverse = 1.0 / jnp.sum(weight, axis=0, keepdims=True)
            prob[group % 2, :, lanes] = unfold(weight * inverse, mask)
            stats[group, 0:1, lanes] = top
            stats[group, 1:2, lanes] = inverse
        grad = dot(prob[group % 2], heads(do, group * GROUP, GROUP), (1, 0))
        hand_out(grad, group, (own, s1, s2, s3, s4))


def score_kernel(
    lengths, q, do, k0, k1, k2, k3, k4, v0, v1, v2, v3, v4, stats, dq, own, s1, s2, s3, s4, bias, dsc
):
    fill_bias(lengths, bias)
    mask = lower()
    for group in range(GROUPS):
        keys, values = blocks((k0, k1, k2, k3, k4), group), blocks((v0, v1, v2, v3, v4), group)
        for pair in range(GROUP // 2):
            lanes = slice(pair * 256, (pair + 1) * 256)
            first = group * GROUP + 2 * pair
            top, inverse = stats[group, 0:1, lanes], stats[group, 1:2, lanes]
            scores = fold(dot(keys, heads(q, first, 2), (1, 1)), mask) + bias[...]
            probability = jnp.exp2((scores - top) * SCALE_LOG2) * inverse
            dprob = fold(dot(values, heads(do, first, 2), (1, 1)), mask)
            delta = jnp.sum(probability.astype(BF16).astype(F32) * dprob, axis=0, keepdims=True)
            dsc[group % 2, :, lanes] = unfold(probability * (dprob - delta), mask)
        rows = (dot(dsc[group % 2], keys, (0, 0)) * SCALE).astype(BF16)
        for n in range(GROUP):
            head = group * GROUP + n
            dq[:, head * HD : (head + 1) * HD] = rows[n * HD : (n + 1) * HD]
        grad = dot(dsc[group % 2], heads(q, group * GROUP, GROUP), (1, 0)) * SCALE
        hand_out(grad, group, (own, s1, s2, s3, s4))


def sds(shape, dtype):
    return jax.ShapeDtypeStruct(shape, dtype)


VMEM = pl.BlockSpec(memory_space=pltpu.VMEM)
SMEM = pl.BlockSpec(memory_space=pltpu.SMEM)
TERMS = [sds((ROWS, GROUPS * HD), F32)] + [sds((ROWS, GROUPS * HD), BF16)] * NEAR
STATS = sds((GROUPS, 8, GROUP * ROWS), F32)
SCRATCH = [pltpu.VMEM((NEAR * ROWS, 2 * ROWS), F32), pltpu.VMEM((2, 5 * ROWS, GROUP * ROWS), BF16)]


def value_call(lengths, value, q, do, keys):
    return pl.pallas_call(
        value_kernel,
        in_specs=[SMEM] + [VMEM] * 8,
        out_specs=[VMEM] * 7,
        out_shape=[sds(value.shape, BF16)] + TERMS + [STATS],
        scratch_shapes=SCRATCH,
        compiler_params=params(24),
        cost_estimate=pl.CostEstimate(flops=15 * 10**10, bytes_accessed=4 * 10**6, transcendentals=2 * 10**6),
        name="value_grad",
    )(lengths, value, q, do, *keys)


def score_call(lengths, q, do, keys, values, stats):
    return pl.pallas_call(
        score_kernel,
        in_specs=[SMEM] + [VMEM] * 13,
        out_specs=[VMEM] * 6,
        out_shape=[sds((ROWS, GROUPS * GROUP * HD), BF16)] + TERMS,
        scratch_shapes=SCRATCH,
        compiler_params=params(24),
        cost_estimate=pl.CostEstimate(flops=4 * 10**10, bytes_accessed=4 * 10**6, transcendentals=2 * 10**6),
        name="score_grad",
    )(lengths, q, do, *keys, *values, stats)


def deal_kernel(x, out, pick):
    step = pl.program_id(0)

    @pl.when(step == 0)
    def _():
        row = lax.broadcasted_iota(jnp.int32, (256, 256), 0)
        col = lax.broadcasted_iota(jnp.int32, (256, 256), 1)
        pick[...] = jnp.where(row == col, 1.0, 0.0).astype(BF16)

    for n in range(4):
        dealt = dot(pick[...], x[:, n * 256 : (n + 1) * 256], (1, 1)).astype(BF16)
        member = (n % 2) * 4 + (step // 4) * 2 + n // 2
        for ctx in range(8):
            first = pl.multiple_of((ctx % 2) * 128 + (step % 4) * 32, 32)
            out[member, ctx // 2, pl.ds(first, 32)] = dealt[ctx * 32 : (ctx + 1) * 32]


def deal_call(x):
    return pl.pallas_call(
        deal_kernel,
        grid=(8,),
        in_specs=[pl.BlockSpec((ROWS, 1024), lambda step: (0, step))],
        out_specs=pl.BlockSpec((8, 4, 256, ROWS), lambda step: (0, 0, 0, 0)),
        out_shape=sds((8, 4, 256, ROWS), BF16),
        scratch_shapes=[pltpu.VMEM((256, 256), BF16)],
        compiler_params=params(24),
        cost_estimate=pl.CostEstimate(flops=2 * 10**9, bytes_accessed=4 * 10**6, transcendentals=0),
        name="deal_inputs",
    )(x)


def weight_kernel(inputs, *refs):
    grads, outs = refs[:8], refs[-4:]
    dp, ctx = lax.axis_index("dp"), lax.axis_index("ctx")
    core, high, low, x = dp % 2, dp // 16, dp // 2 % 2, ctx // 2
    members = [(core ^ c) * 4 + (high ^ h) * 2 + (low ^ n) for c in range(2) for n in range(2) for h in range(2)]
    right = jnp.concatenate([ref[...] for ref in grads], axis=0)
    for n, out in enumerate(outs):
        left = jnp.concatenate([inputs[member, (x + n) % 4] for member in members], axis=1)
        out[...] = dot(left, right, (1, 0)).astype(out.dtype)


def weight_call(inputs, grads, others):
    shape = (256, grads[0].shape[1])
    return pl.pallas_call(
        weight_kernel,
        in_specs=[VMEM] * (9 + len(others)),
        out_specs=[VMEM] * 4,
        out_shape=[sds(shape, F32)] + [sds(shape, BF16)] * 3,
        compiler_params=params(24),
        cost_estimate=pl.CostEstimate(flops=10**6, bytes_accessed=10**4, transcendentals=0),
        name="weight_grad",
    )(inputs, *grads, *others)


def place(device):
    dp, ctx = divmod(device, 8)
    return ctx // 2, dp // 16 * 2 + ctx % 2, dp // 2 % 8, dp % 2


def device(x, y, z, core):
    return ((y // 2 * 8 + z) * 2 + core) * 8 + x * 2 + y % 2


def move(array, dx=0, flip_y=False, flip_z=False, flip_core=False):
    pairs = []
    for source in range(256):
        x, y, z, core = place(source)
        target = device((x + dx) % 4, 3 - y if flip_y else y, z ^ flip_z, core ^ flip_core)
        pairs.append((source, target))
    return lax.ppermute(array, ("dp", "ctx"), pairs)


def ring(array, distance):
    return lax.ppermute(array, "ctx", [(n, (n + distance) % 8) for n in range(8)])


def after(array, *others):
    return lax.optimization_barrier((array, *others))[0]


def shards(query_heads, key_heads, value_heads, out_grad, layer_inputs, doc_lengths):
    q, do = query_heads[0], out_grad[0]
    key, value = key_heads[0], value_heads[0]
    tokens = lax.axis_size("dp") * lax.axis_size("ctx") * q.shape[0]
    keys = [key] + [ring(key, d) for d in range(1, 5)]
    dealt = deal_call(layer_inputs[0])
    members = [
        [device(x, y, z, core) for core in range(2) for y in ys for z in (z0, z0 + 1)]
        for x in range(4)
        for ys in ((1, 2), (0, 3))
        for z0 in range(0, 8, 2)
    ]
    inputs = lax.all_to_all(dealt, ("dp", "ctx"), 0, 0, axis_index_groups=members)

    passed, *value_terms, stats = value_call(doc_lengths, value, q, do, keys)
    values = [value] + [ring(passed, d) for d in range(1, 5)]
    arrived = [ring(term, -d) for d, term in enumerate(value_terms[1:], 1)]
    value_grad = (value_terms[0] + sum(term.astype(F32) for term in arrived)).astype(BF16)

    flips = ((True, False), (False, True), (True, True))
    grads = [value_grad] + [move(value_grad, flip_y=y, flip_z=z) for y, z in flips]
    grads += [move(grad, flip_core=True) for grad in grads]
    total, *away = weight_call(inputs, grads, values[1:])
    across = [move(term, dx=d) for d, term in enumerate(away, 1)]

    query_grad, *key_terms = score_call(doc_lengths, q, do, keys, values, after(stats, total))
    arrived = [ring(term, -d) for d, term in enumerate(key_terms[1:], 1)]
    key_grad = (key_terms[0] + sum(term.astype(F32) for term in arrived)).astype(BF16)
    total = (after(total, query_grad) + sum(term.astype(F32) for term in across)).astype(BF16)
    owners = [
        [device(x, 2 * high + y, 2 * z + low, core) for y in range(2) for z in range(4)]
        for x in range(4)
        for high in range(2)
        for low in range(2)
        for core in range(2)
    ]
    parts = lax.all_to_all(total.reshape(8, 32, -1), ("dp", "ctx"), 0, 0, axis_index_groups=owners)
    weight_grad = jnp.sum(parts.astype(F32), axis=0) * tokens**-0.5

    return query_grad[None], key_grad[None], value_grad[None], weight_grad


def solution(mesh):
    split = P("dp", "ctx", None)
    return jax.shard_map(
        shards,
        mesh=mesh,
        in_specs=(split,) * 5 + (P("dp", None),),
        out_specs=(split, split, split, P(("dp", "ctx"), None)),
        check_vma=False,
    )
```

```python
import functools
import math

import jax
import jax.numpy as jnp
from jax import lax
from jax.experimental import pallas as pl
from jax.experimental.pallas import tpu as pltpu
from jax.sharding import PartitionSpec as P

HD = 128
GROUPS = 4
GROUP = 8
ROWS = 128
NEAR = 4
SCALE = HD**-0.5
SCALE_LOG2 = SCALE * math.log2(math.e)
NEG_FILL = -1e30
F32 = jnp.float32
BF16 = jnp.bfloat16


def params(mib):
    return pltpu.CompilerParams(vmem_limit_bytes=mib * 2**20)


def dot(a, b, contract):
    return lax.dot_general(a, b, ((contract[:1], contract[1:]), ((), ())), preferred_element_type=F32)


def fill_bias(lengths, bias):
    first = lax.axis_index("ctx") * ROWS
    query = lax.broadcasted_iota(jnp.int32, (ROWS, 2 * ROWS), 1) % ROWS
    key = lax.broadcasted_iota(jnp.int32, (ROWS, 2 * ROWS), 0)
    start = jnp.zeros_like(query)
    ending = jnp.int32(0)
    for n in range(lengths.shape[1]):
        ending = ending + lengths[0, n]
        start = jnp.where(ending <= query + first, ending, start)
    for block in range(NEAR):
        place = key + (first - block * ROWS)
        if block == 0:
            place = jnp.where(key <= query, place, place - NEAR * ROWS)
        bias[block * ROWS : (block + 1) * ROWS, :] = jnp.where(place >= start, 0.0, NEG_FILL)


def lower():
    query = lax.broadcasted_iota(jnp.int32, (ROWS, 2 * ROWS), 1) % ROWS
    key = lax.broadcasted_iota(jnp.int32, (ROWS, 2 * ROWS), 0)
    return key <= query


def fold(tile, mask):
    return jnp.concatenate(
        [jnp.where(mask, tile[:ROWS], tile[NEAR * ROWS :]), tile[ROWS : NEAR * ROWS]], axis=0
    )


def unfold(tile, mask):
    return jnp.concatenate(
        [
            jnp.where(mask, tile[:ROWS], 0.0).astype(BF16),
            tile[ROWS:].astype(BF16),
            jnp.where(mask, 0.0, tile[:ROWS]).astype(BF16),
        ],
        axis=0,
    )


def heads(ref, first, count):
    return jnp.concatenate([ref[:, (first + n) * HD : (first + n + 1) * HD] for n in range(count)], axis=0)


def blocks(refs, column):
    return jnp.concatenate([ref[:, column * HD : (column + 1) * HD] for ref in refs], axis=0)


def hand_out(grad, group, outs):
    cols = slice(group * HD, (group + 1) * HD)
    for n, ref in enumerate(outs):
        ref[:, cols] = grad[n * ROWS : (n + 1) * ROWS].astype(ref.dtype)


def value_kernel(lengths, value, q, do, k0, k1, k2, k3, k4, passed, own, s1, s2, s3, s4, stats, bias, prob):
    passed[...] = value[...]
    fill_bias(lengths, bias)
    mask = lower()
    for group in range(GROUPS):
        keys = blocks((k0, k1, k2, k3, k4), group)
        for pair in range(GROUP // 2):
            lanes = slice(pair * 256, (pair + 1) * 256)
            scores = fold(dot(keys, heads(q, group * GROUP + 2 * pair, 2), (1, 1)), mask) + bias[...]
            top = jnp.max(scores, axis=0, keepdims=True)
            weight = jnp.exp2((scores - top) * SCALE_LOG2)
            inverse = 1.0 / jnp.sum(weight, axis=0, keepdims=True)
            prob[group % 2, :, lanes] = unfold(weight * inverse, mask)
            stats[group, 0:1, lanes] = top
            stats[group, 1:2, lanes] = inverse
        grad = dot(prob[group % 2], heads(do, group * GROUP, GROUP), (1, 0))
        hand_out(grad, group, (own, s1, s2, s3, s4))


def score_kernel(
    lengths, q, do, k0, k1, k2, k3, k4, v0, v1, v2, v3, v4, stats, dq, own, s1, s2, s3, s4, bias, dsc
):
    fill_bias(lengths, bias)
    mask = lower()
    for group in range(GROUPS):
        keys, values = blocks((k0, k1, k2, k3, k4), group), blocks((v0, v1, v2, v3, v4), group)
        for pair in range(GROUP // 2):
            lanes = slice(pair * 256, (pair + 1) * 256)
            first = group * GROUP + 2 * pair
            top, inverse = stats[group, 0:1, lanes], stats[group, 1:2, lanes]
            scores = fold(dot(keys, heads(q, first, 2), (1, 1)), mask) + bias[...]
            probability = jnp.exp2((scores - top) * SCALE_LOG2) * inverse
            dprob = fold(dot(values, heads(do, first, 2), (1, 1)), mask)
            delta = jnp.sum(probability.astype(BF16).astype(F32) * dprob, axis=0, keepdims=True)
            dsc[group % 2, :, lanes] = unfold(probability * (dprob - delta), mask)
        rows = (dot(dsc[group % 2], keys, (0, 0)) * SCALE).astype(BF16)
        for n in range(GROUP):
            head = group * GROUP + n
            dq[:, head * HD : (head + 1) * HD] = rows[n * HD : (n + 1) * HD]
        grad = dot(dsc[group % 2], heads(q, group * GROUP, GROUP), (1, 0)) * SCALE
        hand_out(grad, group, (own, s1, s2, s3, s4))


def sds(shape, dtype):
    return jax.ShapeDtypeStruct(shape, dtype)


VMEM = pl.BlockSpec(memory_space=pltpu.VMEM)
SMEM = pl.BlockSpec(memory_space=pltpu.SMEM)
TERMS = [sds((ROWS, GROUPS * HD), F32)] + [sds((ROWS, GROUPS * HD), BF16)] * NEAR
STATS = sds((GROUPS, 8, GROUP * ROWS), F32)
SCRATCH = [pltpu.VMEM((NEAR * ROWS, 2 * ROWS), F32), pltpu.VMEM((2, 5 * ROWS, GROUP * ROWS), BF16)]


def value_call(lengths, value, q, do, keys):
    return pl.pallas_call(
        value_kernel,
        in_specs=[SMEM] + [VMEM] * 8,
        out_specs=[VMEM] * 7,
        out_shape=[sds(value.shape, BF16)] + TERMS + [STATS],
        scratch_shapes=SCRATCH,
        compiler_params=params(24),
        cost_estimate=pl.CostEstimate(flops=15 * 10**10, bytes_accessed=4 * 10**6, transcendentals=2 * 10**6),
        name="value_grad",
    )(lengths, value, q, do, *keys)


def score_call(lengths, q, do, keys, values, stats):
    return pl.pallas_call(
        score_kernel,
        in_specs=[SMEM] + [VMEM] * 13,
        out_specs=[VMEM] * 6,
        out_shape=[sds((ROWS, GROUPS * GROUP * HD), BF16)] + TERMS,
        scratch_shapes=SCRATCH,
        compiler_params=params(58),
        cost_estimate=pl.CostEstimate(flops=4 * 10**10, bytes_accessed=4 * 10**6, transcendentals=2 * 10**6),
        name="score_grad",
    )(lengths, q, do, *keys, *values, stats)


def deal_kernel(x, out, pick):
    step = pl.program_id(0)

    @pl.when(step == 0)
    def _():
        row = lax.broadcasted_iota(jnp.int32, (256, 256), 0)
        col = lax.broadcasted_iota(jnp.int32, (256, 256), 1)
        pick[...] = jnp.where(row == col, 1.0, 0.0).astype(BF16)

    for n in range(4):
        dealt = dot(pick[...], x[:, n * 256 : (n + 1) * 256], (1, 1)).astype(BF16)
        member = (n % 2) * 4 + (step // 4) * 2 + n // 2
        for ctx in range(8):
            first = pl.multiple_of((ctx % 2) * 128 + (step % 4) * 32, 32)
            out[member, ctx // 2, pl.ds(first, 32)] = dealt[ctx * 32 : (ctx + 1) * 32]


def deal_call(x):
    return pl.pallas_call(
        deal_kernel,
        grid=(8,),
        in_specs=[pl.BlockSpec((ROWS, 1024), lambda step: (0, step))],
        out_specs=pl.BlockSpec((8, 4, 256, ROWS), lambda step: (0, 0, 0, 0)),
        out_shape=sds((8, 4, 256, ROWS), BF16),
        scratch_shapes=[pltpu.VMEM((256, 256), BF16)],
        compiler_params=params(24),
        cost_estimate=pl.CostEstimate(flops=2 * 10**9, bytes_accessed=4 * 10**6, transcendentals=0),
        name="deal_inputs",
    )(x)


def weight_kernel(inputs, *refs):
    grads, own, away = refs[:8], refs[-2], refs[-1]
    dp, ctx = lax.axis_index("dp"), lax.axis_index("ctx")
    core, high, low, x = dp % 2, dp // 16, dp // 2 % 2, ctx // 2
    members = [(core ^ c) * 4 + (high ^ h) * 2 + (low ^ n) for c in range(2) for n in range(2) for h in range(2)]
    right = jnp.concatenate([ref[...] for ref in grads], axis=0)
    for n in range(4):
        left = jnp.concatenate([inputs[member, (x + n) % 4] for member in members], axis=1)
        term = dot(left, right, (1, 0))
        for y in range(2):
            away[(x + n) % 4 * 2 + y] = term[y * 128 : (y + 1) * 128].astype(BF16)
        if n == 0:
            own[...] = jnp.where(ctx % 2 == 0, term[:128], term[128:])
    away[ctx] = jnp.zeros(away.shape[1:], BF16)


def weight_call(inputs, grads, others):
    shape = (128, grads[0].shape[1])
    return pl.pallas_call(
        weight_kernel,
        in_specs=[VMEM] * (9 + len(others)),
        out_specs=[VMEM] * 2,
        out_shape=[sds(shape, F32), sds((8, *shape), BF16)],
        compiler_params=params(24),
        cost_estimate=pl.CostEstimate(flops=10**6, bytes_accessed=10**4, transcendentals=0),
        name="weight_grad",
    )(inputs, *grads, *others)


def part_kernel(own, across, *outs):
    total = own[...] + sum(across[n].astype(F32) for n in range(8))
    near = lax.axis_index("dp") // 4 % 4
    for n, out in enumerate(outs):
        rows = total[:32]
        for z in range(1, 4):
            rows = jnp.where((near + n) % 4 == z, total[z * 32 : (z + 1) * 32], rows)
        out[...] = rows.astype(out.dtype)


def part_call(own, across):
    shape = (32, own.shape[1])
    return pl.pallas_call(
        part_kernel,
        in_specs=[VMEM] * 2,
        out_specs=[VMEM] * 4,
        out_shape=[sds(shape, F32)] + [sds(shape, BF16)] * 3,
        compiler_params=params(16),
        cost_estimate=pl.CostEstimate(flops=10**6, bytes_accessed=10**6, transcendentals=0),
        name="add_terms",
    )(own, across)


def place(device):
    dp, ctx = divmod(device, 8)
    return ctx // 2, dp // 16 * 2 + ctx % 2, dp // 2 % 8, dp % 2


def device(x, y, z, core):
    return ((y // 2 * 8 + z) * 2 + core) * 8 + x * 2 + y % 2


def move(array, dz=0, flip_y=False, flip_z=False, flip_core=False):
    pairs = []
    for source in range(256):
        x, y, z, core = place(source)
        target = device(x, 3 - y if flip_y else y, (z ^ flip_z) + dz & 7, core ^ flip_core)
        pairs.append((source, target))
    return lax.ppermute(array, ("dp", "ctx"), pairs)


def ring(array, distance):
    return lax.ppermute(array, "ctx", [(n, (n + distance) % 8) for n in range(8)])


def after(array, *others):
    return lax.optimization_barrier((array, *others))[0]


def shards(query_heads, key_heads, value_heads, out_grad, layer_inputs, doc_lengths):
    q, do = query_heads[0], out_grad[0]
    key, value = key_heads[0], value_heads[0]
    tokens = lax.axis_size("dp") * lax.axis_size("ctx") * q.shape[0]
    keys = [key] + [ring(key, d) for d in range(1, 5)]
    dealt = deal_call(layer_inputs[0])
    members = [
        [device(x, y, z, core) for core in range(2) for y in ys for z in (z0, z0 + 1)]
        for x in range(4)
        for ys in ((1, 2), (0, 3))
        for z0 in range(0, 8, 2)
    ]
    inputs = lax.all_to_all(dealt, ("dp", "ctx"), 0, 0, axis_index_groups=members)

    passed, *value_terms, stats = value_call(doc_lengths, value, q, do, keys)
    values = [value] + [ring(passed, d) for d in range(1, 5)]
    arrived = [ring(term, -d) for d, term in enumerate(value_terms[1:], 1)]
    value_grad = (value_terms[0] + sum(term.astype(F32) for term in arrived)).astype(BF16)

    flips = ((True, False), (False, True), (True, True))
    grads = [value_grad] + [move(value_grad, flip_y=y, flip_z=z) for y, z in flips]
    grads += [move(grad, flip_core=True) for grad in grads]
    total, away = weight_call(inputs, grads, values[1:])
    across = lax.all_to_all(away, "ctx", 0, 0)

    query_grad, *key_terms = score_call(doc_lengths, q, do, keys, values, after(stats, total))
    arrived = [ring(term, -d) for d, term in enumerate(key_terms[1:], 1)]
    key_grad = (key_terms[0] + sum(term.astype(F32) for term in arrived)).astype(BF16)
    total, *away = part_call(after(total, query_grad), across)
    total = total + sum(move(term, dz=2 * d).astype(F32) for d, term in enumerate(away, 1))
    weight_grad = total * tokens**-0.5

    return query_grad[None], key_grad[None], value_grad[None], weight_grad


def solution(mesh):
    split = P("dp", "ctx", None)
    return jax.shard_map(
        shards,
        mesh=mesh,
        in_specs=(split,) * 5 + (P("dp", None),),
        out_specs=(split, split, split, P(("dp", "ctx"), None)),
        check_vma=False,
    )
```

```python
import functools
import math

import jax
import jax.numpy as jnp
from jax import lax
from jax.experimental import pallas as pl
from jax.experimental.pallas import tpu as pltpu
from jax.sharding import PartitionSpec as P

HD = 128
GROUPS = 4
GROUP = 8
ROWS = 128
NEAR = 4
SCALE = HD**-0.5
SCALE_LOG2 = SCALE * math.log2(math.e)
NEG_FILL = -1e30
F32 = jnp.float32
BF16 = jnp.bfloat16


def params(mib):
    return pltpu.CompilerParams(vmem_limit_bytes=mib * 2**20)


def dot(a, b, contract):
    return lax.dot_general(a, b, ((contract[:1], contract[1:]), ((), ())), preferred_element_type=F32)


def fill_bias(lengths, bias):
    first = lax.axis_index("ctx") * ROWS
    query = lax.broadcasted_iota(jnp.int32, (ROWS, 2 * ROWS), 1) % ROWS
    key = lax.broadcasted_iota(jnp.int32, (ROWS, 2 * ROWS), 0)
    start = jnp.zeros_like(query)
    ending = jnp.int32(0)
    for n in range(lengths.shape[1]):
        ending = ending + lengths[0, n]
        start = jnp.where(ending <= query + first, ending, start)
    for block in range(NEAR):
        place = key + (first - block * ROWS)
        if block == 0:
            place = jnp.where(key <= query, place, place - NEAR * ROWS)
        bias[block * ROWS : (block + 1) * ROWS, :] = jnp.where(place >= start, 0.0, NEG_FILL)


def lower():
    query = lax.broadcasted_iota(jnp.int32, (ROWS, 2 * ROWS), 1) % ROWS
    key = lax.broadcasted_iota(jnp.int32, (ROWS, 2 * ROWS), 0)
    return key <= query


def fold(tile, mask):
    return jnp.concatenate(
        [jnp.where(mask, tile[:ROWS], tile[NEAR * ROWS :]), tile[ROWS : NEAR * ROWS]], axis=0
    )


def unfold(tile, mask):
    return jnp.concatenate(
        [
            jnp.where(mask, tile[:ROWS], 0.0).astype(BF16),
            tile[ROWS:].astype(BF16),
            jnp.where(mask, 0.0, tile[:ROWS]).astype(BF16),
        ],
        axis=0,
    )


def heads(ref, first, count):
    return jnp.concatenate([ref[:, (first + n) * HD : (first + n + 1) * HD] for n in range(count)], axis=0)


def blocks(refs, column):
    return jnp.concatenate([ref[:, column * HD : (column + 1) * HD] for ref in refs], axis=0)


def hand_out(grad, group, outs):
    cols = slice(group * HD, (group + 1) * HD)
    for n, ref in enumerate(outs):
        ref[:, cols] = grad[n * ROWS : (n + 1) * ROWS].astype(ref.dtype)


def value_kernel(lengths, value, q, do, k0, k1, k2, k3, k4, passed, own, s1, s2, s3, s4, stats, bias, prob):
    passed[...] = value[...]
    fill_bias(lengths, bias)
    mask = lower()
    for group in range(GROUPS):
        keys = blocks((k0, k1, k2, k3, k4), group)
        for pair in range(GROUP // 2):
            lanes = slice(pair * 256, (pair + 1) * 256)
            scores = fold(dot(keys, heads(q, group * GROUP + 2 * pair, 2), (1, 1)), mask) + bias[...]
            top = jnp.max(scores, axis=0, keepdims=True)
            weight = jnp.exp2((scores - top) * SCALE_LOG2)
            inverse = 1.0 / jnp.sum(weight, axis=0, keepdims=True)
            prob[group % 2, :, lanes] = unfold(weight * inverse, mask)
            stats[group, 0:1, lanes] = top
            stats[group, 1:2, lanes] = inverse
        grad = dot(prob[group % 2], heads(do, group * GROUP, GROUP), (1, 0))
        hand_out(grad, group, (own, s1, s2, s3, s4))


def score_kernel(
    lengths, q, do, k0, k1, k2, k3, k4, v0, v1, v2, v3, v4, stats, dq, own, s1, s2, s3, s4, bias, dsc
):
    @pl.when(pl.program_id(0) == 0)
    def _():
        fill_bias(lengths, bias)

    mask = lower()
    for group in range(GROUPS // 2):
        keys, values = blocks((k0, k1, k2, k3, k4), group), blocks((v0, v1, v2, v3, v4), group)
        for pair in range(GROUP // 2):
            lanes = slice(pair * 256, (pair + 1) * 256)
            first = group * GROUP + 2 * pair
            top, inverse = stats[group, 0:1, lanes], stats[group, 1:2, lanes]
            scores = fold(dot(keys, heads(q, first, 2), (1, 1)), mask) + bias[...]
            probability = jnp.exp2((scores - top) * SCALE_LOG2) * inverse
            dprob = fold(dot(values, heads(do, first, 2), (1, 1)), mask)
            delta = jnp.sum(probability.astype(BF16).astype(F32) * dprob, axis=0, keepdims=True)
            dsc[group % 2, :, lanes] = unfold(probability * (dprob - delta), mask)
        rows = (dot(dsc[group % 2], keys, (0, 0)) * SCALE).astype(BF16)
        for n in range(GROUP):
            head = group * GROUP + n
            dq[:, head * HD : (head + 1) * HD] = rows[n * HD : (n + 1) * HD]
        grad = dot(dsc[group % 2], heads(q, group * GROUP, GROUP), (1, 0)) * SCALE
        hand_out(grad, group, (own, s1, s2, s3, s4))


def sds(shape, dtype):
    return jax.ShapeDtypeStruct(shape, dtype)


VMEM = pl.BlockSpec(memory_space=pltpu.VMEM)
SMEM = pl.BlockSpec(memory_space=pltpu.SMEM)
TERMS = [sds((ROWS, GROUPS * HD), F32)] + [sds((ROWS, GROUPS * HD), BF16)] * NEAR
STATS = sds((GROUPS, 8, GROUP * ROWS), F32)
SCRATCH = [pltpu.VMEM((NEAR * ROWS, 2 * ROWS), F32), pltpu.VMEM((2, 5 * ROWS, GROUP * ROWS), BF16)]


def value_call(lengths, value, q, do, keys):
    return pl.pallas_call(
        value_kernel,
        in_specs=[SMEM] + [VMEM] * 8,
        out_specs=[VMEM] * 7,
        out_shape=[sds(value.shape, BF16)] + TERMS + [STATS],
        scratch_shapes=SCRATCH,
        compiler_params=params(24),
        cost_estimate=pl.CostEstimate(flops=15 * 10**10, bytes_accessed=4 * 10**6, transcendentals=2 * 10**6),
        name="value_grad",
    )(lengths, value, q, do, *keys)


def score_call(lengths, q, do, keys, values, stats):
    def half(width):
        return pl.BlockSpec((ROWS, width), lambda n: (0, n))

    wide, narrow = half(GROUPS // 2 * GROUP * HD), half(GROUPS // 2 * HD)
    return pl.pallas_call(
        score_kernel,
        grid=(2,),
        in_specs=[SMEM, wide, wide]
        + [narrow] * 10
        + [pl.BlockSpec((GROUPS // 2, 8, GROUP * ROWS), lambda n: (n, 0, 0))],
        out_specs=[wide] + [narrow] * 5,
        out_shape=[sds((ROWS, GROUPS * GROUP * HD), BF16)] + TERMS,
        scratch_shapes=SCRATCH,
        compiler_params=params(58),
        cost_estimate=pl.CostEstimate(flops=4 * 10**10, bytes_accessed=4 * 10**6, transcendentals=2 * 10**6),
        name="score_grad",
    )(lengths, q, do, *keys, *values, stats)


def deal_kernel(x, out, pick):
    step = pl.program_id(0)

    @pl.when(step == 0)
    def _():
        row = lax.broadcasted_iota(jnp.int32, (256, 256), 0)
        col = lax.broadcasted_iota(jnp.int32, (256, 256), 1)
        pick[...] = jnp.where(row == col, 1.0, 0.0).astype(BF16)

    for n in range(4):
        dealt = dot(pick[...], x[:, n * 256 : (n + 1) * 256], (1, 1)).astype(BF16)
        member = (n % 2) * 4 + (step // 4) * 2 + n // 2
        for ctx in range(8):
            first = pl.multiple_of((ctx % 2) * 128 + (step % 4) * 32, 32)
            out[member, ctx // 2, pl.ds(first, 32)] = dealt[ctx * 32 : (ctx + 1) * 32]


def deal_call(x):
    return pl.pallas_call(
        deal_kernel,
        grid=(8,),
        in_specs=[pl.BlockSpec((ROWS, 1024), lambda step: (0, step))],
        out_specs=pl.BlockSpec((8, 4, 256, ROWS), lambda step: (0, 0, 0, 0)),
        out_shape=sds((8, 4, 256, ROWS), BF16),
        scratch_shapes=[pltpu.VMEM((256, 256), BF16)],
        compiler_params=params(24),
        cost_estimate=pl.CostEstimate(flops=2 * 10**9, bytes_accessed=4 * 10**6, transcendentals=0),
        name="deal_inputs",
    )(x)


def weight_kernel(inputs, *refs):
    grads, own, away = refs[:8], refs[-2], refs[-1]
    dp, ctx = lax.axis_index("dp"), lax.axis_index("ctx")
    core, high, low, x = dp % 2, dp // 16, dp // 2 % 2, ctx // 2
    members = [(core ^ c) * 4 + (high ^ h) * 2 + (low ^ n) for c in range(2) for n in range(2) for h in range(2)]
    right = jnp.concatenate([ref[...] for ref in grads], axis=0)
    for n in range(4):
        left = jnp.concatenate([inputs[member, (x + n) % 4] for member in members], axis=1)
        term = dot(left, right, (1, 0))
        for y in range(2):
            away[(x + n) % 4 * 2 + y] = term[y * 128 : (y + 1) * 128].astype(BF16)
        if n == 0:
            own[...] = jnp.where(ctx % 2 == 0, term[:128], term[128:])
    away[ctx] = jnp.zeros(away.shape[1:], BF16)


def weight_call(inputs, grads, others):
    shape = (128, grads[0].shape[1])
    return pl.pallas_call(
        weight_kernel,
        in_specs=[VMEM] * (9 + len(others)),
        out_specs=[VMEM] * 2,
        out_shape=[sds(shape, F32), sds((8, *shape), BF16)],
        compiler_params=params(24),
        cost_estimate=pl.CostEstimate(flops=10**6, bytes_accessed=10**4, transcendentals=0),
        name="weight_grad",
    )(inputs, *grads, *others)


def part_kernel(own, across, *outs):
    total = own[...] + sum(across[n].astype(F32) for n in range(8))
    near = lax.axis_index("dp") // 4 % 4
    for n, out in enumerate(outs):
        rows = total[:32]
        for z in range(1, 4):
            rows = jnp.where((near + n) % 4 == z, total[z * 32 : (z + 1) * 32], rows)
        out[...] = rows.astype(out.dtype)


def part_call(own, across):
    shape = (32, own.shape[1])
    return pl.pallas_call(
        part_kernel,
        in_specs=[VMEM] * 2,
        out_specs=[VMEM] * 4,
        out_shape=[sds(shape, F32)] + [sds(shape, BF16)] * 3,
        compiler_params=params(16),
        cost_estimate=pl.CostEstimate(flops=10**6, bytes_accessed=10**6, transcendentals=0),
        name="add_terms",
    )(own, across)


def place(device):
    dp, ctx = divmod(device, 8)
    return ctx // 2, dp // 16 * 2 + ctx % 2, dp // 2 % 8, dp % 2


def device(x, y, z, core):
    return ((y // 2 * 8 + z) * 2 + core) * 8 + x * 2 + y % 2


def move(array, dz=0, flip_y=False, flip_z=False, flip_core=False):
    pairs = []
    for source in range(256):
        x, y, z, core = place(source)
        target = device(x, 3 - y if flip_y else y, (z ^ flip_z) + dz & 7, core ^ flip_core)
        pairs.append((source, target))
    return lax.ppermute(array, ("dp", "ctx"), pairs)


def ring(array, distance):
    return lax.ppermute(array, "ctx", [(n, (n + distance) % 8) for n in range(8)])


def after(array, *others):
    return lax.optimization_barrier((array, *others))[0]


def shards(query_heads, key_heads, value_heads, out_grad, layer_inputs, doc_lengths):
    q, do = query_heads[0], out_grad[0]
    key, value = key_heads[0], value_heads[0]
    tokens = lax.axis_size("dp") * lax.axis_size("ctx") * q.shape[0]
    keys = [key] + [ring(key, d) for d in range(1, 5)]
    dealt = deal_call(layer_inputs[0])
    members = [
        [device(x, y, z, core) for core in range(2) for y in ys for z in (z0, z0 + 1)]
        for x in range(4)
        for ys in ((1, 2), (0, 3))
        for z0 in range(0, 8, 2)
    ]
    inputs = lax.all_to_all(dealt, ("dp", "ctx"), 0, 0, axis_index_groups=members)

    passed, *value_terms, stats = value_call(doc_lengths, value, q, do, keys)
    values = [value] + [ring(passed, d) for d in range(1, 5)]
    arrived = [ring(term, -d) for d, term in enumerate(value_terms[1:], 1)]
    value_grad = (value_terms[0] + sum(term.astype(F32) for term in arrived)).astype(BF16)

    flips = ((True, False), (False, True), (True, True))
    grads = [value_grad] + [move(value_grad, flip_y=y, flip_z=z) for y, z in flips]
    grads += [move(grad, flip_core=True) for grad in grads]
    total, away = weight_call(inputs, grads, values[1:])
    across = lax.all_to_all(away, "ctx", 0, 0)

    query_grad, *key_terms = score_call(doc_lengths, q, do, keys, values, after(stats, total))
    arrived = [ring(term, -d) for d, term in enumerate(key_terms[1:], 1)]
    key_grad = (key_terms[0] + sum(term.astype(F32) for term in arrived)).astype(BF16)
    total, *away = part_call(after(total, query_grad), across)
    total = total + sum(move(term, dz=2 * d).astype(F32) for d, term in enumerate(away, 1))
    weight_grad = total * tokens**-0.5

    return query_grad[None], key_grad[None], value_grad[None], weight_grad


def solution(mesh):
    split = P("dp", "ctx", None)
    return jax.shard_map(
        shards,
        mesh=mesh,
        in_specs=(split,) * 5 + (P("dp", None),),
        out_specs=(split, split, split, P(("dp", "ctx"), None)),
        check_vma=False,
    )
```
